512 devices in a mesh: row: 32 (over x, z_hi, core), col: 16 (over z_lo, y).
Axes of the slice: x: 4, y: 8, z: 8 (z_hi: 4, z_lo: 2; z = z_hi * 2 + z_lo), core: 2. Of those that a mesh axis runs over, the one named last changes fastest.
Arguments:
- tokens: bfloat16 [1152, 8192], P('row', 'col'), may hold values from -6 to 6
- gate_weight: bfloat16 [8192, 28672], P('col', 'row'), may hold values from -0.0625 to 0.0625
- up_weight: bfloat16 [8192, 28672], P('col', 'row'), may hold values from -0.0625 to 0.0625
- down_weight: bfloat16 [28672, 8192], P('row', 'col'), may hold values from -0.03125 to 0.03125
Outputs:
- mixed: bfloat16 [1152, 8192], P('row', 'col')
The draws below stay inside these ranges and needn't reach their ends.
All inputs are finite; a program needn't handle non-finite values.
Results may differ from the reference program's by a relative error of at most 0.005.
Values may be sent and summed in bfloat16 or wider, within the bound.
A program may use at most 64 MiB of HBM per device.

```python
import jax
import jax.numpy as jnp
from jax import lax

D = 8192
FF = 28672
TOKENS = 1152
N_ROW = 32
N_COL = 16


def block_scale(stream_key, dims, split, low, top_value):
    def one(dim, parts):
        heights = jax.random.uniform(jax.random.fold_in(jax.random.fold_in(stream_key, 6), dim), (parts,), jnp.float32, low / len(split), top_value / len(split))
        return jnp.repeat(jnp.exp(heights), dims[dim] // parts).reshape((-1,) + (1,) * (len(dims) - dim - 1))

    gain = one(*split[0])
    for cut in split[1:]:
        gain = gain * one(*cut)
    return gain


def normal_values(rng, shape, deviation, reach, cuts=(), kind=jnp.bfloat16):
    factor_of = block_scale(rng, shape, cuts, -0.22, 0.18) if cuts else 1.0
    entries = jax.random.normal(rng, shape, jnp.float32) * deviation * factor_of
    return jnp.minimum(jnp.maximum(entries, -reach), reach).astype(kind)


def setup_inputs(seed: int = 0) -> dict:
    keys = jax.random.split(jax.random.key(seed), 5)
    return {
        "tokens": normal_values(keys[0], (TOKENS, D), 1.0, 6.0, ((0, 32), (1, 16))),
        "gate_weight": normal_values(keys[1], (D, FF), D ** -0.5, 0.0625, ((0, 16), (1, 32))),
        "up_weight": normal_values(keys[2], (D, FF), D ** -0.5, 0.0625, ((0, 16), (1, 32))),
        "down_weight": normal_values(keys[3], (FF, D), FF ** -0.5, 0.03125, ((0, 32), (1, 16))),
    }


def reference(tokens, gate_weight, up_weight, down_weight):
    feat_group = D // N_COL
    unit_group = FF // N_ROW
    both_weight = jnp.concatenate([gate_weight, up_weight], axis=1)

    def add_feature(total, index):
        start = (index * feat_group).astype(jnp.int32)
        rows_in = lax.dynamic_slice_in_dim(tokens, start, feat_group, 1)
        weight_rows = lax.dynamic_slice_in_dim(both_weight, start, feat_group, 0)
        term = jnp.dot(rows_in, weight_rows, preferred_element_type=jnp.float32)
        return total + term, None

    start_total = jnp.zeros((tokens.shape[0], 2 * FF), jnp.float32)
    both, _ = lax.scan(add_feature, start_total, jnp.arange(N_COL, dtype=jnp.int32))
    gate = both[:, :FF]
    up = both[:, FF:]
    hidden = (jax.nn.silu(gate) * up).astype(jnp.bfloat16)

    def add_units(total, index):
        start = (index * unit_group).astype(jnp.int32)
        cols = lax.dynamic_slice_in_dim(hidden, start, unit_group, 1)
        weight_rows = lax.dynamic_slice_in_dim(down_weight, start, unit_group, 0)
        part = jnp.dot(cols, weight_rows, preferred_element_type=jnp.float32)
        return total + part, None

    out_total = jnp.zeros((tokens.shape[0], D), jnp.float32)
    mixed, _ = lax.scan(add_units, out_total, jnp.arange(N_ROW, dtype=jnp.int32))
    return mixed.astype(jnp.bfloat16)
```

```python
import functools

import jax
import jax.numpy as jnp
from jax import lax
from jax.experimental import pallas as pl
from jax.experimental.pallas import tpu as pltpu
from jax.sharding import PartitionSpec as P

F32, BF16 = jnp.float32, jnp.bfloat16
NX, NY, NZ = 4, 8, 8
TOK = 36
BLK = 144
GRP = 512
NF = 7
NCH = 4
ZTYPE = BF16


def device(x, y, z, c):
    return {"row": (x * 4 + z // 2) * 2 + c, "col": lax.rem(z, 2) * 8 + y}


def kernel(
    tok, gate, up, down, out,
    fs, tz, xf, tx, wgu, dw, sl, slf, ss, ssf, rl, rlf, rs, rsf, hb, xs, xr, xo, zsf, zs, zr,
    tz_s, tz_r, tx_s, tx_r, wl, wz_s, wz_r, wo_s, wo_r, wf_s, wf_r, dl, dz_s, dz_r, do_s, do_r, df_s, df_r,
    rl_s, rl_r, rs_s, rs_r, gl_s, gl_r, gs_s, gs_r, xx_s, xx_r, zz_s, zz_r,
):
    row, col = lax.axis_index("row"), lax.axis_index("col")
    x, zh, c = row // 8, lax.rem(row // 2, 4), lax.rem(row, 2)
    zl, y = col // 8, lax.rem(col, 8)
    z = zh * 2 + zl
    primary = c == zl

    def at(dx=0, dy=0, dz=0):
        return device(lax.rem(x + dx + NX, NX), lax.rem(y + dy + NY, NY), lax.rem(z + dz + NZ, NZ), c)

    other_core = device(x, y, z, 1 - c)
    z_partner = device(x, y, zh * 2 + (1 - zl), c)
    xoff = lambda i: jnp.where(i == 0, 1, jnp.where(i == 1, -1, jnp.where(i == 2, 2, 0)))

    def copy(src, dst, send, recv, where):
        return pltpu.make_async_remote_copy(
            src_ref=src, dst_ref=dst, send_sem=send, recv_sem=recv,
            device_id=where, device_id_type=pl.DeviceIdType.MESH,
        )

    mine = pl.ds(pl.multiple_of(zl * GRP, GRP), GRP)
    theirs = pl.ds(pl.multiple_of((1 - zl) * GRP, GRP), GRP)
    cols = lambda f: pl.ds(pl.multiple_of(f * 128, 128), 128)

    bar = pltpu.get_barrier_semaphore()
    peers = [at(dz=k) for k in range(1, NZ)] + [at(dx=k) for k in range(1, NX)]
    peers += [at(dy=1), at(dy=-1), other_core]
    for p in peers:
        pl.semaphore_signal(bar, inc=1, device_id=p, device_id_type=pl.DeviceIdType.MESH)

    @pl.when(primary)
    def _():
        for f in range(NF):
            pltpu.make_async_copy(gate.at[:, cols(f)], wgu.at[f, mine, pl.ds(0, 128)], wl).start()
            pltpu.make_async_copy(up.at[:, cols(f)], wgu.at[f, mine, pl.ds(128, 128)], wl).start()
        pltpu.make_async_copy(down, dw.at[zl], dl).start()

    t = tok[...].astype(F32)
    for k in range(4):
        fs[k * TOK:(k + 1) * TOK, :] = t[:, k * 128:(k + 1) * 128]
    tz[z] = fs[...].astype(BF16)

    pl.semaphore_wait(bar, len(peers))

    def tz_copy(k):
        return copy(tz.at[z], tz.at[z], tz_s.at[k], tz_r.at[k], at(dz=k))

    for k in (4, 3, 5, 2, 6, 1, 7):
        tz_copy(k).start()

    order = (4, -3, 3, -2, 2, -1, 1, 0)

    def block(offset):
        return lax.rem(y + offset + NY, NY)

    def weight_z(f):
        return (
            copy(gate.at[:, cols(f)], wgu.at[f, mine, pl.ds(0, 128)], wz_s.at[f], wz_r.at[f], z_partner),
            copy(up.at[:, cols(f)], wgu.at[f, mine, pl.ds(128, 128)], wz_s.at[f], wz_r.at[f], z_partner),
        )

    def weight_own(f):
        return (
            copy(gate.at[:, cols(f)], wgu.at[f, mine, pl.ds(0, 128)], wo_s, wo_r, other_core),
            copy(up.at[:, cols(f)], wgu.at[f, mine, pl.ds(128, 128)], wo_s, wo_r, other_core),
        )

    def weight_fwd(f):
        return copy(wgu.at[f, theirs], wgu.at[f, theirs], wf_s.at[f], wf_r.at[f], other_core)

    down_z = copy(down, dw.at[zl], dz_s, dz_r, z_partner)
    down_own = copy(down, dw.at[zl], do_s, do_r, other_core)
    down_fwd = copy(dw.at[1 - zl], dw.at[1 - zl], df_s, df_r, other_core)
    half_all = wgu.at[:, mine]

    @pl.when(jnp.logical_not(primary))
    def _():
        for o in order:
            f = block(o)

            @pl.when(f != NF)
            def _():
                for d in weight_z(f):
                    d.start()
        down_z.start()

    @pl.when(primary)
    def _():
        for f in range(NF):
            for d in weight_own(f):
                d.start()
        down_own.start()

    for k in range(1, NZ):
        pass
    for k in range(1, NZ):
        src = lax.rem(z - k + NZ, NZ)
        copy(tz.at[src], tz.at[src], tz_s.at[k], tz_r.at[k], at(dz=k)).wait_recv()
    for p in range(NZ):
        fs[...] = tz[p].astype(F32)
        for k in range(4):
            lanes = (p % 2) * GRP + k * 128
            xf[(p // 2) * TOK:(p // 2 + 1) * TOK, lanes:lanes + 128] = fs[k * TOK:(k + 1) * TOK, :]
    tx[3] = xf[...].astype(BF16)

    def tx_copy(i):
        return copy(tx.at[3], tx.at[i], tx_s.at[i], tx_r.at[i], at(dx=-(1, -1, 2)[i]))

    for i in range(3):
        tx_copy(i).start()

    @pl.when(primary)
    def _():
        pltpu.make_async_copy(half_all, half_all, wl).wait()

    @pl.when(jnp.logical_not(primary))
    def _():
        copy(half_all, wgu.at[:, theirs], wo_s, wo_r, other_core).wait_recv()

    def turn(i):
        return 1 - 2 * lax.rem(i, 2)

    def product(i, f):
        acc = jnp.dot(tx[i], wgu[f], preferred_element_type=F32)
        return jnp.concatenate([acc[:, :128], acc[:, 128:]], axis=0)

    def take_weights(i, f):
        @pl.when(i == 0)
        def _():
            @pl.when(primary)
            def _():
                copy(wgu.at[f, mine], wgu.at[f, theirs], wz_s.at[f], wz_r.at[f], z_partner).wait_recv()
                weight_fwd(f).start()

            @pl.when(jnp.logical_not(primary))
            def _():
                copy(wgu.at[f, mine], wgu.at[f, mine], wf_s.at[f], wf_r.at[f], other_core).wait_recv()

    def long_copy(i, s):
        to = at(dy=turn(i))
        if s < 3:
            return copy(sl.at[i, s], rl.at[i, s], rl_s.at[i, s], rl_r.at[i, s], to)
        return copy(slf.at[i], rlf.at[i], rl_s.at[i, s], rl_r.at[i, s], to)

    def short_copy(i, s):
        to = at(dy=-turn(i))
        if s < 2:
            return copy(ss.at[i, s], rs.at[i, s], rs_s.at[i, s], rs_r.at[i, s], to)
        return copy(ssf.at[i], rsf.at[i], rs_s.at[i, s], rs_r.at[i, s], to)

    def long_block(i, s):
        return block(turn(i) * (4 - s))

    def short_block(i, s):
        return block(-turn(i) * (3 - s))

    def reduce_step(i, s):
        f = long_block(i, s)

        @pl.when(f != NF)
        def _():
            take_weights(i, f)
            v = product(i, f)
            if s > 0:
                long_copy(i, s - 1).wait_recv()
                v = v + rl[i, s - 1].astype(F32)
            if s < 3:
                sl[i, s] = v.astype(BF16)
            else:
                slf[i] = v
            long_copy(i, s).start()

        if s == 3:
            return
        f2 = short_block(i, s)

        @pl.when(f2 != NF)
        def _():
            take_weights(i, f2)
            v = product(i, f2)
            if s > 0:
                short_copy(i, s - 1).wait_recv()
                v = v + rs[i, s - 1].astype(F32)
            if s < 2:
                ss[i, s] = v.astype(BF16)
            else:
                ssf[i] = v
            short_copy(i, s).start()

    def gather_long(i, s, f):
        return copy(hb.at[i, f], hb.at[i, f], gl_s.at[i, s], gl_r.at[i, s], at(dy=turn(i)))

    def gather_short(i, s, f):
        return copy(hb.at[i, f], hb.at[i, f], gs_s.at[i, s], gs_r.at[i, s], at(dy=-turn(i)))

    def finish(i):
        @pl.when(y != NF)
        def _():
            take_weights(i, y)
            v = product(i, y)
            long_copy(i, 3).wait_recv()
            short_copy(i, 2).wait_recv()
            v = v + rlf[i] + rsf[i]
            g, u = v[:BLK], v[BLK:]
            hb[i, y] = (g / (1.0 + jnp.exp(-g)) * u).astype(BF16)
            gather_long(i, 0, y).start()
            gather_short(i, 0, y).start()

    def gather_step(i, s):
        f = block(-turn(i) * s)

        @pl.when(f != NF)
        def _():
            gather_long(i, s - 1, f).wait_recv()
            gather_long(i, s, f).start()

        if s == 3:
            return
        f2 = block(turn(i) * s)

        @pl.when(f2 != NF)
        def _():
            gather_short(i, s - 1, f2).wait_recv()
            gather_short(i, s, f2).start()

    def x_copy(i):
        return copy(xs.at[i], xr.at[i], xx_s.at[i], xx_r.at[i], at(dx=xoff(i)))

    def project(i):
        f = block(-turn(i) * 4)

        @pl.when(f != NF)
        def _():
            gather_long(i, 3, f).wait_recv()

        f2 = block(turn(i) * 3)

        @pl.when(f2 != NF)
        def _():
            gather_short(i, 2, f2).wait_recv()

        f3 = block(turn(i) * 3)

        @pl.when(i == 0)
        def _():
            @pl.when(primary)
            def _():
                pltpu.make_async_copy(down, dw.at[zl], dl).wait()
                copy(down, dw.at[1 - zl], dz_s, dz_r, z_partner).wait_recv()
                down_fwd.start()

            @pl.when(jnp.logical_not(primary))
            def _():
                copy(down, dw.at[zl], do_s, do_r, other_core).wait_recv()
                copy(down, dw.at[1 - zl], df_s, df_r, other_core).wait_recv()

        h = jnp.concatenate([hb[i, f] for f in range(NF)], axis=1)
        for half in range(2):
            v = jnp.dot(h, dw[half], preferred_element_type=F32)
            lanes = slice(half * GRP, (half + 1) * GRP)

            @pl.when(i < 3)
            def _():
                xs[jnp.minimum(i, 2), :, lanes] = v.astype(BF16)

            @pl.when(i == 3)
            def _():
                xo[:, lanes] = v

        @pl.when(i < 3)
        def _():
            x_copy(jnp.minimum(i, 2)).start()

    stages = [functools.partial(reduce_step, s=s) for s in range(4)]
    stages += [finish] + [functools.partial(gather_step, s=s) for s in (1, 2, 3)] + [project]

    def slot(t, carry):
        for s in reversed(range(len(stages))):
            i = t - s

            @pl.when(jnp.logical_and(i >= 0, i < NCH))
            def _():
                @pl.when(jnp.logical_and(s == 0, jnp.logical_and(i >= 0, i < 3)))
                def _():
                    j = jnp.minimum(i, 2)
                    copy(tx.at[3], tx.at[j], tx_s.at[j], tx_r.at[j], at(dx=-xoff(j))).wait_recv()

                stages[s](i)
        return carry

    lax.fori_loop(0, NCH + len(stages) - 1, slot, 0)

    for i in range(3):
        x_copy(i).wait_recv()
    xf[...] = xo[...] + xr[0].astype(F32) + xr[1].astype(F32) + xr[2].astype(F32)
    for p in range(NZ):
        for k in range(4):
            lanes = (p % 2) * GRP + k * 128
            fs[k * TOK:(k + 1) * TOK, :] = xf[(p // 2) * TOK:(p // 2 + 1) * TOK, lanes:lanes + 128]
        v = fs[...]
        zsf[p] = v
        zs[p] = v.astype(ZTYPE)

    def z_copy(k):
        to = lax.rem(z + k, NZ)
        return copy(zs.at[to], zr.at[k], zz_s.at[k], zz_r.at[k], at(dz=k))

    for k in (4, 3, 5, 2, 6, 1, 7):
        z_copy(k).start()
    v = zsf[z]
    for k in (1, 7, 2, 6, 3, 5, 4):
        z_copy(k).wait_recv()
        v = v + zr[k].astype(F32)
    fs[...] = v
    for k in range(4):
        out[:, k * 128:(k + 1) * 128] = fs[k * TOK:(k + 1) * TOK, :].astype(BF16)

    for k in range(1, NZ):
        tz_copy(k).wait_send()
        z_copy(k).wait_send()
    for i in range(3):
        tx_copy(i).wait_send()
        x_copy(i).wait_send()

    @pl.when(primary)
    def _():
        copy(half_all, half_all, wo_s, wo_r, other_core).wait_send()
        down_own.wait_send()
        down_fwd.wait_send()
        for f in range(NF):
            weight_fwd(f).wait_send()

    @pl.when(jnp.logical_not(primary))
    def _():
        for f in range(NF):
            copy(wgu.at[f, mine], wgu.at[f, mine], wz_s.at[f], wz_r.at[f], z_partner).wait_send()
        down_z.wait_send()

    def drain(i, carry):
        for s in range(4):
            f = long_block(i, s)

            @pl.when(f != NF)
            def _():
                long_copy(i, s).wait_send()

            f = block(-turn(i) * s)

            @pl.when(f != NF)
            def _():
                gather_long(i, s, f).wait_send()

        for s in range(3):
            f = short_block(i, s)

            @pl.when(f != NF)
            def _():
                short_copy(i, s).wait_send()

            f = block(turn(i) * s)

            @pl.when(f != NF)
            def _():
                gather_short(i, s, f).wait_send()

        return carry

    lax.fori_loop(0, NCH, drain, 0)


def per_device(tokens, gate_weight, up_weight, down_weight):
    vmem, dma = pltpu.VMEM, pltpu.SemaphoreType.DMA
    scratch = [
        vmem((BLK, 128), F32),
        vmem((NZ, BLK, 128), BF16),
        vmem((BLK, 2 * GRP), F32),
        vmem((NCH, BLK, 2 * GRP), BF16),
        vmem((NF, 2 * GRP, 256), BF16),
        vmem((2, NF * 128, GRP), BF16),
        vmem((NCH, 3, 2 * BLK, 128), BF16),
        vmem((NCH, 2 * BLK, 128), F32),
        vmem((NCH, 2, 2 * BLK, 128), BF16),
        vmem((NCH, 2 * BLK, 128), F32),
        vmem((NCH, 3, 2 * BLK, 128), BF16),
        vmem((NCH, 2 * BLK, 128), F32),
        vmem((NCH, 2, 2 * BLK, 128), BF16),
        vmem((NCH, 2 * BLK, 128), F32),
        vmem((NCH, NF, BLK, 128), BF16),
        vmem((3, BLK, 2 * GRP), BF16),
        vmem((3, BLK, 2 * GRP), BF16),
        vmem((BLK, 2 * GRP), F32),
        vmem((NZ, BLK, 128), F32),
        vmem((NZ, BLK, 128), ZTYPE),
        vmem((NZ, BLK, 128), ZTYPE),
        dma((NZ,)), dma((NZ,)), dma((3,)), dma((3,)),
        dma, dma((NF,)), dma((NF,)), dma, dma, dma((NF,)), dma((NF,)),
        dma, dma, dma, dma, dma, dma, dma,
        dma((NCH, 4)), dma((NCH, 4)), dma((NCH, 3)), dma((NCH, 3)),
        dma((NCH, 4)), dma((NCH, 4)), dma((NCH, 3)), dma((NCH, 3)),
        dma((3,)), dma((3,)), dma((NZ,)), dma((NZ,)),
    ]
    return pl.pallas_call(
        kernel,
        out_shape=jax.ShapeDtypeStruct(tokens.shape, BF16),
        in_specs=[pl.BlockSpec(memory_space=pltpu.VMEM)] + [pl.BlockSpec(memory_space=pl.ANY)] * 3,
        out_specs=pl.BlockSpec(memory_space=pltpu.VMEM),
        scratch_shapes=scratch,
        compiler_params=pltpu.CompilerParams(
            collective_id=0, has_side_effects=True, vmem_limit_bytes=48 * 2**20
        ),
    )(tokens, gate_weight, up_weight, down_weight)


def solution(mesh):
    in_specs = (P("row", "col"), P("col", "row"), P("col", "row"), P("row", "col"))
    return jax.shard_map(
        per_device, mesh=mesh, in_specs=in_specs, out_specs=P("row", "col"), check_vma=False
    )
```

```python
import functools

import jax
import jax.numpy as jnp
from jax import lax
from jax.experimental import pallas as pl
from jax.experimental.pallas import tpu as pltpu
from jax.sharding import PartitionSpec as P

F32, BF16 = jnp.float32, jnp.bfloat16
NX, NY, NZ = 4, 8, 8
TOK = 36
BLK = 144
GRP = 512
NF = 7
NCH = 4


def device(x, y, z, c):
    return {"row": (x * 4 + z // 2) * 2 + c, "col": lax.rem(z, 2) * 8 + y}


def kernel(
    tok, gate, up, down, out,
    tv, fs, tk, xf, tx, ws, ds, wgu, dw, msg_out, msg_in, hb, zsf, zs, zr,
    tl, tz_s, tz_r, tx_s, tx_r, wl, wz_s, wz_r, wo_s, wo_r, wf_s, wf_r, dl, dz_s, dz_r, do_s, do_r, df_s, df_r,
    ra_s, ra_r, ga_s, ga_r, zz_s, zz_r,
):
    row, col = lax.axis_index("row"), lax.axis_index("col")
    x, zh, c = row // 8, lax.rem(row // 2, 4), lax.rem(row, 2)
    zl, y = col // 8, lax.rem(col, 8)
    z = zh * 2 + zl
    primary = c == zl
    secondary = c != zl

    def at(dx=0, dy=0, dz=0):
        return device(lax.rem(x + dx + NX, NX), lax.rem(y + dy + NY, NY), lax.rem(z + dz + NZ, NZ), c)

    other_core = device(x, y, z, 1 - c)
    z_partner = device(x, y, zh * 2 + (1 - zl), c)
    xoff = lambda i: (2, 1, -1, 0)[i] if isinstance(i, int) else jnp.where(i == 0, 2, jnp.where(i == 1, 1, jnp.where(i == 2, -1, 0)))

    def copy(src, dst, send, recv, where):
        return pltpu.make_async_remote_copy(
            src_ref=src, dst_ref=dst, send_sem=send, recv_sem=recv,
            device_id=where, device_id_type=pl.DeviceIdType.MESH,
        )

    mine = pl.ds(pl.multiple_of(zl * GRP, GRP), GRP)
    theirs = pl.ds(pl.multiple_of((1 - zl) * GRP, GRP), GRP)
    cols = lambda f: pl.ds(pl.multiple_of(f * 128, 128), 128)

    def block(offset):
        return lax.rem(y + offset + NY, NY)

    bar = pltpu.get_barrier_semaphore()
    peers = [at(dz=k) for k in (4, 3, 5, 2, 6)] + [at(dx=2), at(dy=2), at(dy=-2)]
    peers += [at(dz=1), at(dz=-1), at(dx=1), at(dx=-1), at(dy=1), at(dy=-1), other_core]
    for p in peers:
        pl.semaphore_signal(bar, inc=1, device_id=p, device_id_type=pl.DeviceIdType.MESH)

    tokens = pltpu.make_async_copy(tok, tv, tl)
    tokens.start()

    @pl.when(primary)
    def _():
        for f in range(NF):
            pltpu.make_async_copy(gate.at[:, cols(f)], wgu.at[f, mine, pl.ds(0, 128)], wl).start()
            pltpu.make_async_copy(up.at[:, cols(f)], wgu.at[f, mine, pl.ds(128, 128)], wl).start()
        pltpu.make_async_copy(down, dw.at[zl], dl).start()

    @pl.when(secondary)
    def _():
        for f in range(NF):
            pltpu.make_async_copy(gate.at[:, cols(f)], ws.at[f, :, pl.ds(0, 128)], wl).start()
            pltpu.make_async_copy(up.at[:, cols(f)], ws.at[f, :, pl.ds(128, 128)], wl).start()
        pltpu.make_async_copy(down, ds, dl).start()

    tokens.wait()
    t = tv[...].astype(F32)
    for k in range(4):
        fs[k * TOK:(k + 1) * TOK, :] = t[:, k * 128:(k + 1) * 128]
    tk[3, z] = fs[...].astype(BF16)

    pl.semaphore_wait(bar, len(peers))

    def tz_copy(k):
        return copy(tk.at[3, z], tk.at[3, z], tz_s.at[k], tz_r.at[k], at(dz=k))

    def tx_copy(i, p):
        return copy(tk.at[3, p], tk.at[i, p], tx_s.at[i], tx_r.at[i], at(dx=-(2, 1, -1)[i]))

    for k in (1, 7, 2, 6, 3, 5, 4):
        tz_copy(k).start()
    for i in (1, 2):
        tx_copy(i, z).start()

    order = (4, 3, -3, 1, -1, 2, -2, 0)

    def weight_z(f):
        return copy(ws.at[f], wgu.at[f, mine], wz_s.at[f], wz_r.at[f], z_partner)

    def weight_own(f):
        return copy(wgu.at[f, mine], wgu.at[f, mine], wo_s, wo_r, other_core)

    def weight_fwd(f):
        return copy(wgu.at[f, theirs], wgu.at[f, theirs], wf_s.at[f], wf_r.at[f], other_core)

    down_z = copy(ds, dw.at[zl], dz_s, dz_r, z_partner)
    down_own = copy(dw.at[zl], dw.at[zl], do_s, do_r, other_core)
    down_fwd = copy(dw.at[1 - zl], dw.at[1 - zl], df_s, df_r, other_core)
    half_all = wgu.at[:, mine]

    def piece(k):
        src = lax.rem(z - k + NZ, NZ)
        copy(tk.at[3, src], tk.at[3, src], tz_s.at[k], tz_r.at[k], at(dz=k)).wait_recv()
        for i in (1, 2):
            tx_copy(i, src).start()

    def piece_far(k):
        tx_copy(0, lax.rem(z - k + NZ, NZ)).start()

    piece(1)
    piece(7)
    piece_far(0)

    @pl.when(secondary)
    def _():
        pltpu.make_async_copy(ws, ws, wl).wait()
        pltpu.make_async_copy(ds, ds, dl).wait()
        for o in order:
            f = block(o)

            @pl.when(f != NF)
            def _():
                weight_z(f).start()
        down_z.start()

    @pl.when(primary)
    def _():
        pltpu.make_async_copy(half_all, half_all, wl).wait()
        for f in range(NF):
            weight_own(f).start()
        pltpu.make_async_copy(ds, dw.at[zl], dl).wait()
        down_own.start()

    for ks, behind in (((2, 6), (1, 7)), ((3, 5), (2, 6)), ((4,), (3, 5, 4))):
        for k in ks:
            piece(k)
        for k in behind:
            piece_far(k)

    def assemble(i):
        for p in range(NZ):
            fs[...] = tk[i, p].astype(F32)
            for k in range(4):
                lanes = (p % 2) * GRP + k * 128
                xf[(p // 2) * TOK:(p // 2 + 1) * TOK, lanes:lanes + 128] = fs[k * TOK:(k + 1) * TOK, :]
        tx[i] = xf[...].astype(BF16)

    assemble(3)

    @pl.when(secondary)
    def _():
        copy(half_all, wgu.at[:, theirs], wo_s, wo_r, other_core).wait_recv()

    def turn(i):
        return 1 - 2 * (i % 2) if isinstance(i, int) else 1 - 2 * lax.rem(i, 2)

    def product(i, f):
        acc = jnp.dot(tx[i], wgu[f], preferred_element_type=F32)
        return jnp.concatenate([acc[:, :128], acc[:, 128:]], axis=0)

    def take_weights(*offsets):
        for o in offsets:
            f = block(o)

            @pl.when(jnp.logical_and(f != NF, primary))
            def _():
                copy(wgu.at[f, mine], wgu.at[f, theirs], wz_s.at[f], wz_r.at[f], z_partner).wait_recv()
                weight_fwd(f).start()

            @pl.when(jnp.logical_and(f != NF, secondary))
            def _():
                copy(wgu.at[f, mine], wgu.at[f, mine], wf_s.at[f], wf_r.at[f], other_core).wait_recv()

    def aside(i):
        return NF - 2 * i

    def unit(i, b):
        return jnp.where(b == NF, aside(i), b)

    def message(i, n, to):
        return copy(msg_out.at[n, i], msg_in.at[n, i], ra_s.at[i, n], ra_r.at[i, n], at(dy=turn(i) * to))

    MESSAGES = ((4, 2), (3, 1), (-3, -1), (1, 1), (-1, -1), (2, 2), (-2, -2))

    def send_term(i, n):
        b = block(turn(i) * MESSAGES[n][0])

        @pl.when(jnp.logical_and(b != NF, b != aside(i)))
        def _():
            msg_out[n, i] = product(i, b).astype(BF16)
            message(i, n, MESSAGES[n][1]).start()

    def send_term_moved(i):
        o = lax.rem(turn(i) * (NF - y) + NY, NY)
        n = jnp.where(o == 4, 0, jnp.where(o == 3, 1, jnp.where(o == 5, 2, jnp.where(o == 1, 3, 4))))
        to = jnp.where(o == 4, 2, jnp.where(o == 3, 1, jnp.where(o == 1, 1, -1)))

        @pl.when(jnp.logical_and(lax.rem(o + 2, 4) != 0, lax.rem(o + 8, 8) != 0))
        def _():
            @pl.when(aside(i) != NF)
            def _():
                msg_out[n, i] = product(i, aside(i)).astype(BF16)
                message(i, n, to).start()

    def send_sum(i, n, parts):
        b = block(turn(i) * MESSAGES[n][0])

        @pl.when(b != aside(i))
        def _():
            v = product(i, unit(i, b))
            for m in parts:
                message(i, m, MESSAGES[m][1]).wait_recv()
                v = v + msg_in[m, i].astype(F32)
            msg_out[n, i] = v.astype(BF16)
            message(i, n, MESSAGES[n][1]).start()

    def early(i, s):
        for n in ((0,), (1, 2), (3, 4))[s]:
            send_term(i, n)

    def tokens_of(i):
        copy(tk.at[3], tk.at[i], tx_s.at[i], tx_r.at[i], at(dx=-xoff(i))).wait_recv()
        assemble(i)

    def gather(i, n):
        d = turn(i)
        b, to = ((0, 1), (0, -1), (0, 2), (0, -2), (-2, 1), (-2, 2), (2, -1))[n]
        b = block(d * b)
        f = lax.rem(unit(i, b), NY)
        return b != aside(i), f, lambda: copy(hb.at[i, f], hb.at[i, f], ga_s.at[i, n], ga_r.at[i, n], at(dy=d * to))

    def gather_wait(i, n):
        b = block(turn(i) * (-1, 1, -2, 2, -3, -4, 3)[n])

        @pl.when(b != aside(i))
        def _():
            f = unit(i, b)
            copy(hb.at[i, f], hb.at[i, f], ga_s.at[i, n], ga_r.at[i, n], at(dy=turn(i))).wait_recv()

    def gather_start(i, n):
        ok, _, make = gather(i, n)

        @pl.when(ok)
        def _():
            make().start()

    def finish(i):
        @pl.when(y != aside(i))
        def _():
            f = unit(i, y)
            v = product(i, f)
            for n in (3, 4, 5, 6):
                message(i, n, 1).wait_recv()
                v = v + msg_in[n, i].astype(F32)
            g, u = v[:BLK], v[BLK:]
            hb[i, f] = (g / (1.0 + jnp.exp(-g)) * u).astype(BF16)
            for n in (2, 3, 0, 1):
                gather(i, n)[2]().start()

    def gather_on(i):
        gather_wait(i, 2)
        gather_start(i, 5)
        gather_start(i, 4)
        gather_wait(i, 3)
        gather_start(i, 6)

    def out_copy(i, k):
        src = zs.at[i, lax.rem(z + k, NZ)]
        return copy(src, zr.at[i, k], zz_s.at[i, k], zz_r.at[i, k], at(dx=xoff(i), dz=k))

    def project(i):
        for n in (0, 1, 4, 5, 6):
            gather_wait(i, n)

        @pl.when(i == 0)
        def _():
            @pl.when(primary)
            def _():
                copy(ds, dw.at[1 - zl], dz_s, dz_r, z_partner).wait_recv()
                down_fwd.start()

            @pl.when(secondary)
            def _():
                copy(ds, dw.at[zl], do_s, do_r, other_core).wait_recv()
                copy(ds, dw.at[1 - zl], df_s, df_r, other_core).wait_recv()

        h = jnp.concatenate([hb[i, f] for f in range(NF)], axis=1)
        for half in range(2):
            v = jnp.dot(h, dw[half], preferred_element_type=F32)
            xf[:, half * GRP:(half + 1) * GRP] = v
        for p in range(NZ):
            for k in range(4):
                lanes = (p % 2) * GRP + k * 128
                fs[k * TOK:(k + 1) * TOK, :] = xf[(p // 2) * TOK:(p // 2 + 1) * TOK, lanes:lanes + 128]
            v = fs[...]
            zs[i, p] = v.astype(BF16)

            @pl.when(i == 3)
            def _():
                zsf[p] = v

        for k in (4, 3, 5, 2, 6, 1, 7):
            out_copy(i, k).start()

        @pl.when(i != 3)
        def _():
            out_copy(i, 0).start()

    def over_chunks(body, low=0, high=NCH):
        def step(j, carry):
            body(j)
            return carry

        lax.fori_loop(low, high, step, 0)

    take_weights(4)
    early(3, 0)
    for i in (1, 2, 0):
        tokens_of(i)
    over_chunks(lambda j: early(j, 0), 0, 3)
    take_weights(3, -3)
    over_chunks(lambda j: early(j, 1))
    take_weights(1, -1)
    over_chunks(lambda j: early(j, 2))
    take_weights(2, -2, 0)
    over_chunks(send_term_moved, 1)

    def sums(i):
        send_sum(i, 5, (0, 1))
        send_sum(i, 6, (2,))

    stages = ((sums, 0), (finish, 1), (gather_on, 2), (project, 3))

    def slot(t, carry):
        for stage, s in stages:
            i = t - s

            @pl.when(jnp.logical_and(i >= 0, i < NCH))
            def _():
                stage(i)
        return carry

    lax.fori_loop(0, NCH + 3, slot, 0)

    def add(i, v):
        for k in (0, 1, 7, 2, 6, 3, 5, 4):
            if i != 3 or k > 0:
                out_copy(i, k).wait_recv()
                v = v + zr[i, k].astype(F32)
        return v

    v = zsf[z]
    for i in range(NCH):
        v = add(i, v)
    fs[...] = v
    for k in range(4):
        out[:, k * 128:(k + 1) * 128] = fs[k * TOK:(k + 1) * TOK, :].astype(BF16)

    for k in range(1, NZ):
        tz_copy(k).wait_send()
    for i in range(3):
        copy(tk.at[3], tk.at[i], tx_s.at[i], tx_r.at[i], at(dx=-(2, 1, -1)[i])).wait_send()
    for i in range(NCH):
        for k in range(i // 3, NZ):
            out_copy(i, k).wait_send()

    @pl.when(primary)
    def _():
        copy(half_all, half_all, wo_s, wo_r, other_core).wait_send()
        down_own.wait_send()
        down_fwd.wait_send()
        for f in range(NF):
            weight_fwd(f).wait_send()

    @pl.when(secondary)
    def _():
        for f in range(NF):
            copy(wgu.at[f, mine], wgu.at[f, mine], wz_s.at[f], wz_r.at[f], z_partner).wait_send()
        down_z.wait_send()

    def drain(i, carry):
        for n in range(7):
            b = block(turn(i) * MESSAGES[n][0])

            @pl.when(b != aside(i))
            def _():
                message(i, n, 1).wait_send()

            ok, _, make = gather(i, n)

            @pl.when(ok)
            def _():
                make().wait_send()

        return carry

    lax.fori_loop(0, NCH, drain, 0)


def per_device(tokens, gate_weight, up_weight, down_weight):
    vmem, dma = pltpu.VMEM, pltpu.SemaphoreType.DMA
    scratch = [
        vmem((TOK, GRP), BF16),
        vmem((BLK, 128), F32),
        vmem((NCH, NZ, BLK, 128), BF16),
        vmem((BLK, 2 * GRP), F32),
        vmem((NCH, BLK, 2 * GRP), BF16),
        vmem((NF, GRP, 256), BF16),
        vmem((NF * 128, GRP), BF16),
        vmem((NF, 2 * GRP, 256), BF16),
        vmem((2, NF * 128, GRP), BF16),
        vmem((7, NCH, 2 * BLK, 128), BF16),
        vmem((7, NCH, 2 * BLK, 128), BF16),
        vmem((NCH, NF, BLK, 128), BF16),
        vmem((NZ, BLK, 128), F32),
        vmem((NCH, NZ, BLK, 128), BF16),
        vmem((NCH, NZ, BLK, 128), BF16),
        dma, dma((NZ,)), dma((NZ,)), dma((3,)), dma((3,)),
        dma, dma((NF,)), dma((NF,)), dma, dma, dma((NF,)), dma((NF,)),
        dma, dma, dma, dma, dma, dma, dma,
        dma((NCH, 7)), dma((NCH, 7)), dma((NCH, 7)), dma((NCH, 7)),
        dma((NCH, NZ)), dma((NCH, NZ)),
    ]
    return pl.pallas_call(
        kernel,
        out_shape=jax.ShapeDtypeStruct(tokens.shape, BF16),
        in_specs=[pl.BlockSpec(memory_space=pl.ANY)] * 4,
        out_specs=pl.BlockSpec(memory_space=pltpu.VMEM),
        scratch_shapes=scratch,
        compiler_params=pltpu.CompilerParams(
            collective_id=0, has_side_effects=True, vmem_limit_bytes=63 * 2**20
        ),
    )(tokens, gate_weight, up_weight, down_weight)


def solution(mesh):
    in_specs = (P("row", "col"), P("col", "row"), P("col", "row"), P("row", "col"))
    return jax.shard_map(
        per_device, mesh=mesh, in_specs=in_specs, out_specs=P("row", "col"), check_vma=False
    )
```

```python
import functools

import jax
import jax.numpy as jnp
from jax import lax
from jax.experimental import pallas as pl
from jax.experimental.pallas import tpu as pltpu
from jax.sharding import PartitionSpec as P

F32, BF16 = jnp.float32, jnp.bfloat16
NX, NY, NZ = 4, 8, 8
TOK = 36
BLK = 144
GRP = 512
NF = 7
NCH = 4


def device(x, y, z, c):
    return {"row": (x * 4 + z // 2) * 2 + c, "col": lax.rem(z, 2) * 8 + y}


def kernel(
    tok, gate, up, down, out,
    tv, fs, tk, xf, tx, ws, ds, wgu, dw, msg_out, msg_in, hb, xs, xr, xo, zsf, zs, zr,
    tl, tz_s, tz_r, tx_s, tx_r, wl, wz_s, wz_r, wo_s, wo_r, wf_s, wf_r, dl, dz_s, dz_r, do_s, do_r, df_s, df_r,
    ra_s, ra_r, ga_s, ga_r, xx_s, xx_r, zz_s, zz_r,
):
    row, col = lax.axis_index("row"), lax.axis_index("col")
    x, zh, c = row // 8, lax.rem(row // 2, 4), lax.rem(row, 2)
    zl, y = col // 8, lax.rem(col, 8)
    z = zh * 2 + zl
    primary = c == zl
    secondary = c != zl

    def at(dx=0, dy=0, dz=0):
        return device(lax.rem(x + dx + NX, NX), lax.rem(y + dy + NY, NY), lax.rem(z + dz + NZ, NZ), c)

    other_core = device(x, y, z, 1 - c)
    z_partner = device(x, y, zh * 2 + (1 - zl), c)
    xoff = lambda i: (2, 1, -1, 0)[i] if isinstance(i, int) else jnp.where(i == 0, 2, jnp.where(i == 1, 1, jnp.where(i == 2, -1, 0)))

    def copy(src, dst, send, recv, where):
        return pltpu.make_async_remote_copy(
            src_ref=src, dst_ref=dst, send_sem=send, recv_sem=recv,
            device_id=where, device_id_type=pl.DeviceIdType.MESH,
        )

    mine = pl.ds(pl.multiple_of(zl * GRP, GRP), GRP)
    theirs = pl.ds(pl.multiple_of((1 - zl) * GRP, GRP), GRP)
    cols = lambda f: pl.ds(pl.multiple_of(f * 128, 128), 128)

    def block(offset):
        return lax.rem(y + offset + NY, NY)

    bar = pltpu.get_barrier_semaphore()
    peers = [at(dz=k) for k in (4, 3, 5, 2, 6)] + [at(dx=2), at(dy=2), at(dy=-2)]
    peers += [at(dz=1), at(dz=-1), at(dx=1), at(dx=-1), at(dy=1), at(dy=-1), other_core]
    for p in peers:
        pl.semaphore_signal(bar, inc=1, device_id=p, device_id_type=pl.DeviceIdType.MESH)

    tokens = pltpu.make_async_copy(tok, tv, tl)
    tokens.start()

    @pl.when(primary)
    def _():
        for f in range(NF):
            pltpu.make_async_copy(gate.at[:, cols(f)], wgu.at[f, mine, pl.ds(0, 128)], wl).start()
            pltpu.make_async_copy(up.at[:, cols(f)], wgu.at[f, mine, pl.ds(128, 128)], wl).start()
        pltpu.make_async_copy(down, dw.at[zl], dl).start()

    @pl.when(secondary)
    def _():
        for f in range(NF):
            pltpu.make_async_copy(gate.at[:, cols(f)], ws.at[f, :, pl.ds(0, 128)], wl).start()
            pltpu.make_async_copy(up.at[:, cols(f)], ws.at[f, :, pl.ds(128, 128)], wl).start()
        pltpu.make_async_copy(down, ds, dl).start()

    tokens.wait()
    t = tv[...].astype(F32)
    for k in range(4):
        fs[k * TOK:(k + 1) * TOK, :] = t[:, k * 128:(k + 1) * 128]
    tk[3, z] = fs[...].astype(BF16)

    pl.semaphore_wait(bar, len(peers))

    def tz_copy(k):
        return copy(tk.at[3, z], tk.at[3, z], tz_s.at[k], tz_r.at[k], at(dz=k))

    def tx_copy(i, p):
        return copy(tk.at[3, p], tk.at[i, p], tx_s.at[i], tx_r.at[i], at(dx=-(2, 1, -1)[i]))

    order = (4, 3, -3, 1, -1, 2, -2, 0)

    def weight_z(f):
        return copy(ws.at[f], wgu.at[f, mine], wz_s.at[f], wz_r.at[f], z_partner)

    def weight_own(f):
        return copy(wgu.at[f, mine], wgu.at[f, mine], wo_s, wo_r, other_core)

    def weight_fwd(f):
        return copy(wgu.at[f, theirs], wgu.at[f, theirs], wf_s.at[f], wf_r.at[f], other_core)

    down_z = copy(ds, dw.at[zl], dz_s, dz_r, z_partner)
    down_own = copy(dw.at[zl], dw.at[zl], do_s, do_r, other_core)
    down_fwd = copy(dw.at[1 - zl], dw.at[1 - zl], df_s, df_r, other_core)
    half_all = wgu.at[:, mine]

    for k in (1, 7, 2, 6, 3, 5, 4):
        tz_copy(k).start()
    for i in (1, 2):
        tx_copy(i, z).start()

    @pl.when(secondary)
    def _():
        pltpu.make_async_copy(ws, ws, wl).wait()
        pltpu.make_async_copy(ds, ds, dl).wait()
        for o in order:
            f = block(o)

            @pl.when(f != NF)
            def _():
                weight_z(f).start()
        down_z.start()

    @pl.when(primary)
    def _():
        pltpu.make_async_copy(half_all, half_all, wl).wait()
        for f in range(NF):
            weight_own(f).start()
        pltpu.make_async_copy(ds, dw.at[zl], dl).wait()
        down_own.start()

    def piece(k):
        src = lax.rem(z - k + NZ, NZ)
        copy(tk.at[3, src], tk.at[3, src], tz_s.at[k], tz_r.at[k], at(dz=k)).wait_recv()
        for i in (1, 2):
            tx_copy(i, src).start()

    def piece_far(k):
        tx_copy(0, lax.rem(z - k + NZ, NZ)).start()

    piece(1)
    piece(7)
    piece_far(0)

    for ks, behind in (((2, 6), (1, 7)), ((3, 5), (2, 6)), ((4,), (3, 5, 4))):
        for k in ks:
            piece(k)
        for k in behind:
            piece_far(k)

    def assemble(i):
        for p in range(NZ):
            fs[...] = tk[i, p].astype(F32)
            for k in range(4):
                lanes = (p % 2) * GRP + k * 128
                xf[(p // 2) * TOK:(p // 2 + 1) * TOK, lanes:lanes + 128] = fs[k * TOK:(k + 1) * TOK, :]
        tx[i] = xf[...].astype(BF16)

    assemble(3)

    @pl.when(secondary)
    def _():
        copy(half_all, wgu.at[:, theirs], wo_s, wo_r, other_core).wait_recv()

    def turn(i):
        return 1 - 2 * (i % 2) if isinstance(i, int) else 1 - 2 * lax.rem(i, 2)

    def product(i, f):
        acc = jnp.dot(tx[i], wgu[f], preferred_element_type=F32)
        return jnp.concatenate([acc[:, :128], acc[:, 128:]], axis=0)

    def take_weights(*offsets):
        for o in offsets:
            f = block(o)

            @pl.when(jnp.logical_and(f != NF, primary))
            def _():
                copy(wgu.at[f, mine], wgu.at[f, theirs], wz_s.at[f], wz_r.at[f], z_partner).wait_recv()
                weight_fwd(f).start()

            @pl.when(jnp.logical_and(f != NF, secondary))
            def _():
                copy(wgu.at[f, mine], wgu.at[f, mine], wf_s.at[f], wf_r.at[f], other_core).wait_recv()

    def aside(i):
        return NF - 2 * i

    def unit(i, b):
        return jnp.where(b == NF, aside(i), b)

    def message(i, n, to):
        return copy(msg_out.at[n, i], msg_in.at[n, i], ra_s.at[i, n], ra_r.at[i, n], at(dy=turn(i) * to))

    MESSAGES = ((4, 1), (3, 1), (-3, -1), (1, 1), (-1, -1), (2, 2), (-2, -1))

    def send_term(i, n):
        b = block(turn(i) * MESSAGES[n][0])

        @pl.when(jnp.logical_and(b != NF, b != aside(i)))
        def _():
            msg_out[n, i] = product(i, b).astype(BF16)
            message(i, n, MESSAGES[n][1]).start()

    def send_term_moved(i):
        o = lax.rem(turn(i) * (NF - y) + NY, NY)
        n = jnp.where(o == 4, 0, jnp.where(o == 5, 2, jnp.where(o == 1, 3, 4)))
        to = jnp.where((o == 4) | (o == 1), 1, -1)

        @pl.when(((o == 4) | (o == 5) | (o == 1)) & (aside(i) != NF))
        def _():
            msg_out[n, i] = product(i, aside(i)).astype(BF16)
            message(i, n, to).start()

    def send_sum(i, n, parts):
        b = block(turn(i) * MESSAGES[n][0])

        @pl.when(b != aside(i))
        def _():
            v = product(i, unit(i, b))
            for m in parts:
                message(i, m, MESSAGES[m][1]).wait_recv()
                v = v + msg_in[m, i].astype(F32)
            msg_out[n, i] = v.astype(BF16)
            message(i, n, MESSAGES[n][1]).start()

    def early(i, s):
        for n in (0, 2, 3)[s:s + 1]:
            send_term(i, n)

    def tokens_of(i):
        copy(tk.at[3], tk.at[i], tx_s.at[i], tx_r.at[i], at(dx=-xoff(i))).wait_recv()
        assemble(i)

    def gather(i, n):
        d = turn(i)
        b, to = ((0, 1), (0, -1), (0, 2), (0, -2), (-2, 1), (-2, 2), (2, -1))[n]
        b = block(d * b)
        f = lax.rem(unit(i, b), NY)
        return b != aside(i), f, lambda: copy(hb.at[i, f], hb.at[i, f], ga_s.at[i, n], ga_r.at[i, n], at(dy=d * to))

    def gather_wait(i, n):
        b = block(turn(i) * (-1, 1, -2, 2, -3, -4, 3)[n])

        @pl.when(b != aside(i))
        def _():
            f = unit(i, b)
            copy(hb.at[i, f], hb.at[i, f], ga_s.at[i, n], ga_r.at[i, n], at(dy=turn(i))).wait_recv()

    def gather_start(i, n):
        ok, _, make = gather(i, n)

        @pl.when(ok)
        def _():
            make().start()

    def finish(i):
        @pl.when(y != aside(i))
        def _():
            f = unit(i, y)
            v = product(i, f)
            for n in (3, 4, 5):
                message(i, n, 1).wait_recv()
                v = v + msg_in[n, i].astype(F32)
            g, u = v[:BLK], v[BLK:]
            hb[i, f] = (g / (1.0 + jnp.exp(-g)) * u).astype(BF16)
            for n in (2, 3, 0, 1):
                gather(i, n)[2]().start()

    def gather_on(i):
        gather_wait(i, 2)
        gather_start(i, 5)
        gather_start(i, 4)
        gather_wait(i, 3)
        gather_start(i, 6)

    def x_copy(i):
        return copy(xs.at[i], xr.at[i], xx_s.at[i], xx_r.at[i], at(dx=xoff(i)))

    def project(i):
        for n in (0, 1, 4, 5, 6):
            gather_wait(i, n)

        @pl.when(i == 0)
        def _():
            @pl.when(primary)
            def _():
                copy(ds, dw.at[1 - zl], dz_s, dz_r, z_partner).wait_recv()
                down_fwd.start()

            @pl.when(secondary)
            def _():
                copy(ds, dw.at[zl], do_s, do_r, other_core).wait_recv()
                copy(ds, dw.at[1 - zl], df_s, df_r, other_core).wait_recv()

        h = jnp.concatenate([hb[i, f] for f in range(NF)], axis=1)
        for half in range(2):
            v = jnp.dot(h, dw[half], preferred_element_type=F32)
            xf[:, half * GRP:(half + 1) * GRP] = v
            lanes = slice(half * GRP, (half + 1) * GRP)


        @pl.when((i == 1))
        def _():
            j = jnp.minimum(i, 2)
            xs[j] = xf[...].astype(BF16)
            x_copy(j).start()

        @pl.when((i == 0) | (i == 2))
        def _():
            j = jnp.minimum(i, 2)
            split(lambda p, v: put(zs, j, p, v))
            for k in (4, 3, 5, 2, 6, 0, 1, 7):
                z_copy(j, k).start()

        @pl.when(i == 3)
        def _():
            xo[...] = xf[...]

    def split(store):
        for p in range(NZ):
            for k in range(4):
                lanes = (p % 2) * GRP + k * 128
                fs[k * TOK:(k + 1) * TOK, :] = xf[(p // 2) * TOK:(p // 2 + 1) * TOK, lanes:lanes + 128]
            store(p, fs[...])

    def put(ref, j, p, v):
        ref[j, p] = v.astype(BF16)

    def put_own(p, v):
        zsf[p] = v
        zs[3, p] = v.astype(BF16)

    def z_copy(i, k):
        return copy(zs.at[i, lax.rem(z + k, NZ)], zr.at[i, k], zz_s.at[i, k], zz_r.at[i, k], at(dx=xoff(i), dz=k))

    def over_chunks(body, low=0, high=NCH):
        def step(j, carry):
            body(j)
            return carry

        lax.fori_loop(low, high, step, 0)

    take_weights(4)
    early(3, 0)
    for i in (1, 2, 0):
        tokens_of(i)
    over_chunks(lambda j: early(j, 0), 0, 3)
    take_weights(3, -3)
    over_chunks(lambda j: early(j, 1))
    take_weights(1, -1)
    over_chunks(lambda j: early(j, 2))
    take_weights(2, -2, 0)
    over_chunks(send_term_moved, 1)

    def first_sums(i):
        send_sum(i, 1, (0,))
        send_sum(i, 6, (2,))

    def sums(i):
        send_sum(i, 5, (1,))
        send_sum(i, 4, (6,))

    over_chunks(first_sums)

    stages = ((sums, 0), (finish, 1), (gather_on, 2), (project, 3))

    def slot(t, carry):
        for stage, s in stages:
            i = t - s

            @pl.when(jnp.logical_and(i >= 0, i < NCH))
            def _():
                stage(i)
        return carry

    lax.fori_loop(0, NCH + 3, slot, 0)

    v = xo[...]
    for i in (1,):
        x_copy(i).wait_recv()
        v = v + xr[i].astype(F32)
    xf[...] = v
    split(put_own)
    for k in (4, 3, 5, 2, 6, 1, 7):
        z_copy(3, k).start()
    v = zsf[z]
    for i in (0, 2, 3):
        for k in (0, 1, 7, 2, 6, 3, 5, 4):
            if i != 3 or k > 0:
                z_copy(i, k).wait_recv()
                v = v + zr[i, k].astype(F32)
    fs[...] = v
    for k in range(4):
        out[:, k * 128:(k + 1) * 128] = fs[k * TOK:(k + 1) * TOK, :].astype(BF16)

    for k in range(1, NZ):
        tz_copy(k).wait_send()
        z_copy(3, k).wait_send()
    for i in range(3):
        copy(tk.at[3], tk.at[i], tx_s.at[i], tx_r.at[i], at(dx=-(2, 1, -1)[i])).wait_send()
    for i in (1,):
        x_copy(i).wait_send()
    for i in (0, 2):
        for k in range(NZ):
            z_copy(i, k).wait_send()

    @pl.when(primary)
    def _():
        copy(half_all, half_all, wo_s, wo_r, other_core).wait_send()
        down_own.wait_send()
        down_fwd.wait_send()
        for f in range(NF):
            weight_fwd(f).wait_send()

    @pl.when(secondary)
    def _():
        for f in range(NF):
            copy(wgu.at[f, mine], wgu.at[f, mine], wz_s.at[f], wz_r.at[f], z_partner).wait_send()
        down_z.wait_send()

    def drain(i, carry):
        for n in range(7):
            b = block(turn(i) * MESSAGES[n][0])

            @pl.when(b != aside(i))
            def _():
                message(i, n, 1).wait_send()

            ok, _, make = gather(i, n)

            @pl.when(ok)
            def _():
                make().wait_send()

        return carry

    lax.fori_loop(0, NCH, drain, 0)


def per_device(tokens, gate_weight, up_weight, down_weight):
    vmem, dma = pltpu.VMEM, pltpu.SemaphoreType.DMA
    scratch = [
        vmem((TOK, GRP), BF16),
        vmem((BLK, 128), F32),
        vmem((NCH, NZ, BLK, 128), BF16),
        vmem((BLK, 2 * GRP), F32),
        vmem((NCH, BLK, 2 * GRP), BF16),
        vmem((NF, GRP, 256), BF16),
        vmem((NF * 128, GRP), BF16),
        vmem((NF, 2 * GRP, 256), BF16),
        vmem((2, NF * 128, GRP), BF16),
        vmem((7, NCH, 2 * BLK, 128), BF16),
        vmem((7, NCH, 2 * BLK, 128), BF16),
        vmem((NCH, NF, BLK, 128), BF16),
        vmem((3, BLK, 2 * GRP), BF16),
        vmem((3, BLK, 2 * GRP), BF16),
        vmem((BLK, 2 * GRP), F32),
        vmem((NZ, BLK, 128), F32),
        vmem((NCH, NZ, BLK, 128), BF16),
        vmem((NCH, NZ, BLK, 128), BF16),
        dma, dma((NZ,)), dma((NZ,)), dma((3,)), dma((3,)),
        dma, dma((NF,)), dma((NF,)), dma, dma, dma((NF,)), dma((NF,)),
        dma, dma, dma, dma, dma, dma, dma,
        dma((NCH, 7)), dma((NCH, 7)), dma((NCH, 7)), dma((NCH, 7)),
        dma((3,)), dma((3,)), dma((NCH, NZ)), dma((NCH, NZ)),
    ]
    return pl.pallas_call(
        kernel,
        out_shape=jax.ShapeDtypeStruct(tokens.shape, BF16),
        in_specs=[pl.BlockSpec(memory_space=pl.ANY)] * 4,
        out_specs=pl.BlockSpec(memory_space=pltpu.VMEM),
        scratch_shapes=scratch,
        compiler_params=pltpu.CompilerParams(
            collective_id=0, has_side_effects=True, vmem_limit_bytes=63 * 2**20
        ),
    )(tokens, gate_weight, up_weight, down_weight)


def solution(mesh):
    in_specs = (P("row", "col"), P("col", "row"), P("col", "row"), P("row", "col"))
    return jax.shard_map(
        per_device, mesh=mesh, in_specs=in_specs, out_specs=P("row", "col"), check_vma=False
    )
```

```python
import functools

import jax
import jax.numpy as jnp
from jax import lax
from jax.experimental import pallas as pl
from jax.experimental.pallas import tpu as pltpu
from jax.sharding import PartitionSpec as P

F32, BF16 = jnp.float32, jnp.bfloat16
NX, NY, NZ = 4, 8, 8
TOK = 36
BLK = 144
GRP = 512
NF = 7
NCH = 4


def device(x, y, z, c):
    return {"row": (x * 4 + z // 2) * 2 + c, "col": lax.rem(z, 2) * 8 + y}


def kernel(
    tok, gate, up, down, out,
    tv, fs, tk, xf, tx, ws, ds, wgu, dw, msg_out, msg_in, hb, xs, xr, xo, zsf, zs, zr,
    tl, tz_s, tz_r, tx_s, tx_r, wl, wz_s, wz_r, wo_s, wo_r, wf_s, wf_r, dl, dz_s, dz_r, do_s, do_r, df_s, df_r,
    ra_s, ra_r, ga_s, ga_r, xx_s, xx_r, zz_s, zz_r,
):
    row, col = lax.axis_index("row"), lax.axis_index("col")
    x, zh, c = row // 8, lax.rem(row // 2, 4), lax.rem(row, 2)
    zl, y = col // 8, lax.rem(col, 8)
    z = zh * 2 + zl
    primary = c == zl
    secondary = c != zl

    def at(dx=0, dy=0, dz=0):
        return device(lax.rem(x + dx + NX, NX), lax.rem(y + dy + NY, NY), lax.rem(z + dz + NZ, NZ), c)

    other_core = device(x, y, z, 1 - c)
    z_partner = device(x, y, zh * 2 + (1 - zl), c)
    xoff = lambda i: (2, 1, -1, 0)[i] if isinstance(i, int) else jnp.where(i == 0, 2, jnp.where(i == 1, 1, jnp.where(i == 2, -1, 0)))

    def copy(src, dst, send, recv, where):
        return pltpu.make_async_remote_copy(
            src_ref=src, dst_ref=dst, send_sem=send, recv_sem=recv,
            device_id=where, device_id_type=pl.DeviceIdType.MESH,
        )

    mine = pl.ds(pl.multiple_of(zl * GRP, GRP), GRP)
    theirs = pl.ds(pl.multiple_of((1 - zl) * GRP, GRP), GRP)
    cols = lambda f: pl.ds(pl.multiple_of(f * 128, 128), 128)

    def block(offset):
        return lax.rem(y + offset + NY, NY)

    bar = pltpu.get_barrier_semaphore()
    peers = [at(dz=k) for k in (4, 3, 5, 2, 6)] + [at(dx=2), at(dy=2), at(dy=-2)]
    peers += [at(dz=1), at(dz=-1), at(dx=1), at(dx=-1), at(dy=1), at(dy=-1), other_core]
    for p in peers:
        pl.semaphore_signal(bar, inc=1, device_id=p, device_id_type=pl.DeviceIdType.MESH)

    tokens = pltpu.make_async_copy(tok, tv, tl)
    tokens.start()

    @pl.when(primary)
    def _():
        for f in range(NF):
            pltpu.make_async_copy(gate.at[:, cols(f)], wgu.at[f, mine, pl.ds(0, 128)], wl).start()
            pltpu.make_async_copy(up.at[:, cols(f)], wgu.at[f, mine, pl.ds(128, 128)], wl).start()
        pltpu.make_async_copy(down, dw.at[zl], dl).start()

    @pl.when(secondary)
    def _():
        for f in range(NF):
            pltpu.make_async_copy(gate.at[:, cols(f)], ws.at[f, :, pl.ds(0, 128)], wl).start()
            pltpu.make_async_copy(up.at[:, cols(f)], ws.at[f, :, pl.ds(128, 128)], wl).start()
        pltpu.make_async_copy(down, ds, dl).start()

    tokens.wait()
    t = tv[...].astype(F32)
    for k in range(4):
        fs[k * TOK:(k + 1) * TOK, :] = t[:, k * 128:(k + 1) * 128]
    tk[3, z] = fs[...].astype(BF16)

    pl.semaphore_wait(bar, len(peers))

    def tz_copy(k):
        return copy(tk.at[3, z], tk.at[3, z], tz_s.at[k], tz_r.at[k], at(dz=k))

    def tx_copy(i, p):
        return copy(tk.at[3, p], tk.at[i, p], tx_s.at[i], tx_r.at[i], at(dx=-(2, 1, -1)[i]))

    order = (4, 3, -3, 1, -1, 2, -2, 0)

    def weight_z(f):
        return copy(ws.at[f], wgu.at[f, mine], wz_s.at[f], wz_r.at[f], z_partner)

    def weight_own(f):
        return copy(wgu.at[f, mine], wgu.at[f, mine], wo_s, wo_r, other_core)

    def weight_fwd(f):
        return copy(wgu.at[f, theirs], wgu.at[f, theirs], wf_s.at[f], wf_r.at[f], other_core)

    down_z = copy(ds, dw.at[zl], dz_s, dz_r, z_partner)
    down_own = copy(dw.at[zl], dw.at[zl], do_s, do_r, other_core)
    down_fwd = copy(dw.at[1 - zl], dw.at[1 - zl], df_s, df_r, other_core)
    half_all = wgu.at[:, mine]

    for k in (1, 7, 2, 6, 3, 5, 4):
        tz_copy(k).start()
    for i in (1, 2):
        tx_copy(i, z).start()

    @pl.when(secondary)
    def _():
        pltpu.make_async_copy(ws, ws, wl).wait()
        pltpu.make_async_copy(ds, ds, dl).wait()
        for o in order:
            f = block(o)

            @pl.when(f != NF)
            def _():
                weight_z(f).start()
        down_z.start()

    @pl.when(primary)
    def _():
        pltpu.make_async_copy(half_all, half_all, wl).wait()
        for f in range(NF):
            weight_own(f).start()
        pltpu.make_async_copy(ds, dw.at[zl], dl).wait()
        down_own.start()

    def piece(k):
        src = lax.rem(z - k + NZ, NZ)
        copy(tk.at[3, src], tk.at[3, src], tz_s.at[k], tz_r.at[k], at(dz=k)).wait_recv()
        for i in (1, 2):
            tx_copy(i, src).start()

    def piece_far(k):
        tx_copy(0, lax.rem(z - k + NZ, NZ)).start()

    piece(1)
    piece(7)
    piece_far(0)

    for ks, behind in (((2, 6), (1, 7)), ((3, 5), (2, 6)), ((4,), (3, 5, 4))):
        for k in ks:
            piece(k)
        for k in behind:
            piece_far(k)

    def assemble(i):
        for p in range(NZ):
            fs[...] = tk[i, p].astype(F32)
            for k in range(4):
                lanes = (p % 2) * GRP + k * 128
                xf[(p // 2) * TOK:(p // 2 + 1) * TOK, lanes:lanes + 128] = fs[k * TOK:(k + 1) * TOK, :]
        tx[i] = xf[...].astype(BF16)

    assemble(3)

    @pl.when(secondary)
    def _():
        copy(half_all, wgu.at[:, theirs], wo_s, wo_r, other_core).wait_recv()

    def turn(i):
        return 1 - 2 * (i % 2) if isinstance(i, int) else 1 - 2 * lax.rem(i, 2)

    def product(i, f):
        acc = jnp.dot(tx[i], wgu[f], preferred_element_type=F32)
        return jnp.concatenate([acc[:, :128], acc[:, 128:]], axis=0)

    def take_weights(*offsets):
        for o in offsets:
            f = block(o)

            @pl.when(jnp.logical_and(f != NF, primary))
            def _():
                copy(wgu.at[f, mine], wgu.at[f, theirs], wz_s.at[f], wz_r.at[f], z_partner).wait_recv()
                weight_fwd(f).start()

            @pl.when(jnp.logical_and(f != NF, secondary))
            def _():
                copy(wgu.at[f, mine], wgu.at[f, mine], wf_s.at[f], wf_r.at[f], other_core).wait_recv()

    def aside(i):
        return NF - 2 * i

    def unit(i, b):
        return jnp.where(b == NF, aside(i), b)

    def message(i, n, to):
        return copy(msg_out.at[n, i], msg_in.at[n, i], ra_s.at[i, n], ra_r.at[i, n], at(dy=turn(i) * to))

    MESSAGES = ((4, 2), (3, 1), (-3, -1), (1, 1), (-1, -1), (2, 2), (-2, -2))

    def send_term(i, n):
        b = block(turn(i) * MESSAGES[n][0])

        @pl.when(jnp.logical_and(b != NF, b != aside(i)))
        def _():
            msg_out[n, i] = product(i, b).astype(BF16)
            message(i, n, MESSAGES[n][1]).start()

    def send_term_moved(i):
        o = lax.rem(turn(i) * (NF - y) + NY, NY)
        n = jnp.where(o == 4, 0, jnp.where(o == 3, 1, jnp.where(o == 5, 2, jnp.where(o == 1, 3, 4))))
        to = jnp.where(o == 4, 2, jnp.where(o == 3, 1, jnp.where(o == 1, 1, -1)))

        @pl.when(jnp.logical_and(lax.rem(o + 2, 4) != 0, lax.rem(o + 8, 8) != 0))
        def _():
            @pl.when(aside(i) != NF)
            def _():
                msg_out[n, i] = product(i, aside(i)).astype(BF16)
                message(i, n, to).start()

    def send_sum(i, n, parts):
        b = block(turn(i) * MESSAGES[n][0])

        @pl.when(b != aside(i))
        def _():
            v = product(i, unit(i, b))
            for m in parts:
                message(i, m, MESSAGES[m][1]).wait_recv()
                v = v + msg_in[m, i].astype(F32)
            msg_out[n, i] = v.astype(BF16)
            message(i, n, MESSAGES[n][1]).start()

    def early(i, s):
        for n in ((0,), (1, 2), (3, 4))[s]:
            send_term(i, n)

    def tokens_of(i):
        copy(tk.at[3], tk.at[i], tx_s.at[i], tx_r.at[i], at(dx=-xoff(i))).wait_recv()
        assemble(i)

    def gather(i, n):
        d = turn(i)
        b, to = ((0, 1), (0, -1), (0, 2), (0, -2), (-2, 1), (-2, 2), (2, -1))[n]
        b = block(d * b)
        f = lax.rem(unit(i, b), NY)
        return b != aside(i), f, lambda: copy(hb.at[i, f], hb.at[i, f], ga_s.at[i, n], ga_r.at[i, n], at(dy=d * to))

    def gather_wait(i, n):
        b = block(turn(i) * (-1, 1, -2, 2, -3, -4, 3)[n])

        @pl.when(b != aside(i))
        def _():
            f = unit(i, b)
            copy(hb.at[i, f], hb.at[i, f], ga_s.at[i, n], ga_r.at[i, n], at(dy=turn(i))).wait_recv()

    def gather_start(i, n):
        ok, _, make = gather(i, n)

        @pl.when(ok)
        def _():
            make().start()

    def finish(i):
        @pl.when(y != aside(i))
        def _():
            f = unit(i, y)
            v = product(i, f)
            for n in (3, 4, 5, 6):
                message(i, n, 1).wait_recv()
                v = v + msg_in[n, i].astype(F32)
            g, u = v[:BLK], v[BLK:]
            hb[i, f] = (g / (1.0 + jnp.exp(-g)) * u).astype(BF16)
            for n in (2, 3, 0, 1):
                gather(i, n)[2]().start()

    def gather_on(i):
        gather_wait(i, 2)
        gather_start(i, 5)
        gather_start(i, 4)
        gather_wait(i, 3)
        gather_start(i, 6)

    def x_copy(i):
        return copy(xs.at[i], xr.at[i], xx_s.at[i], xx_r.at[i], at(dx=xoff(i)))

    def project(i):
        for n in (0, 1, 4, 5, 6):
            gather_wait(i, n)

        @pl.when(i == 0)
        def _():
            @pl.when(primary)
            def _():
                copy(ds, dw.at[1 - zl], dz_s, dz_r, z_partner).wait_recv()
                down_fwd.start()

            @pl.when(secondary)
            def _():
                copy(ds, dw.at[zl], do_s, do_r, other_core).wait_recv()
                copy(ds, dw.at[1 - zl], df_s, df_r, other_core).wait_recv()

        h = jnp.concatenate([hb[i, f] for f in range(NF)], axis=1)
        for half in range(2):
            v = jnp.dot(h, dw[half], preferred_element_type=F32)
            xf[:, half * GRP:(half + 1) * GRP] = v
            lanes = slice(half * GRP, (half + 1) * GRP)


        @pl.when((i == 0) | (i == 1))
        def _():
            j = jnp.minimum(i, 2)
            xs[j] = xf[...].astype(BF16)
            x_copy(j).start()

        @pl.when((i == 2))
        def _():
            j = 2
            split(lambda p, v: put(zs, j, p, v))
            for k in (4, 3, 5, 2, 6, 0, 1, 7):
                z_copy(j, k).start()

        @pl.when(i == 3)
        def _():
            xo[...] = xf[...]

    def split(store):
        for p in range(NZ):
            for k in range(4):
                lanes = (p % 2) * GRP + k * 128
                fs[k * TOK:(k + 1) * TOK, :] = xf[(p // 2) * TOK:(p // 2 + 1) * TOK, lanes:lanes + 128]
            store(p, fs[...])

    def put(ref, j, p, v):
        ref[j, p] = v.astype(BF16)

    def put_own(p, v):
        zsf[p] = v
        zs[3, p] = v.astype(BF16)

    def z_copy(i, k):
        return copy(zs.at[i, lax.rem(z + k, NZ)], zr.at[i, k], zz_s.at[i, k], zz_r.at[i, k], at(dx=xoff(i), dz=k))

    def over_chunks(body, low=0, high=NCH):
        def step(j, carry):
            body(j)
            return carry

        lax.fori_loop(low, high, step, 0)

    take_weights(4)
    early(3, 0)
    for i in (1, 2, 0):
        tokens_of(i)
    over_chunks(lambda j: early(j, 0), 0, 3)
    take_weights(3, -3)
    over_chunks(lambda j: early(j, 1))
    take_weights(1, -1)
    over_chunks(lambda j: early(j, 2))
    take_weights(2, -2, 0)
    over_chunks(send_term_moved, 1)

    def sums(i):
        send_sum(i, 5, (0, 1))
        send_sum(i, 6, (2,))

    stages = ((sums, 0), (finish, 1), (gather_on, 2), (project, 3))

    def slot(t, carry):
        for stage, s in stages:
            i = t - s

            @pl.when(jnp.logical_and(i >= 0, i < NCH))
            def _():
                stage(i)
        return carry

    lax.fori_loop(0, NCH + 3, slot, 0)

    v = xo[...]
    for i in (0, 1):
        x_copy(i).wait_recv()
        v = v + xr[i].astype(F32)
    xf[...] = v
    split(put_own)
    for k in (4, 3, 5, 2, 6, 1, 7):
        z_copy(3, k).start()
    v = zsf[z]
    for i in (2, 3):
        for k in (0, 1, 7, 2, 6, 3, 5, 4):
            if i != 3 or k > 0:
                z_copy(i, k).wait_recv()
                v = v + zr[i, k].astype(F32)
    fs[...] = v
    for k in range(4):
        out[:, k * 128:(k + 1) * 128] = fs[k * TOK:(k + 1) * TOK, :].astype(BF16)

    for k in range(1, NZ):
        tz_copy(k).wait_send()
        z_copy(3, k).wait_send()
    for i in range(3):
        copy(tk.at[3], tk.at[i], tx_s.at[i], tx_r.at[i], at(dx=-(2, 1, -1)[i])).wait_send()
    for i in (0, 1):
        x_copy(i).wait_send()
    for i in (2,):
        for k in range(NZ):
            z_copy(i, k).wait_send()

    @pl.when(primary)
    def _():
        copy(half_all, half_all, wo_s, wo_r, other_core).wait_send()
        down_own.wait_send()
        down_fwd.wait_send()
        for f in range(NF):
            weight_fwd(f).wait_send()

    @pl.when(secondary)
    def _():
        for f in range(NF):
            copy(wgu.at[f, mine], wgu.at[f, mine], wz_s.at[f], wz_r.at[f], z_partner).wait_send()
        down_z.wait_send()

    def drain(i, carry):
        for n in range(7):
            b = block(turn(i) * MESSAGES[n][0])

            @pl.when(b != aside(i))
            def _():
                message(i, n, 1).wait_send()

            ok, _, make = gather(i, n)

            @pl.when(ok)
            def _():
                make().wait_send()

        return carry

    lax.fori_loop(0, NCH, drain, 0)


def per_device(tokens, gate_weight, up_weight, down_weight):
    vmem, dma = pltpu.VMEM, pltpu.SemaphoreType.DMA
    scratch = [
        vmem((TOK, GRP), BF16),
        vmem((BLK, 128), F32),
        vmem((NCH, NZ, BLK, 128), BF16),
        vmem((BLK, 2 * GRP), F32),
        vmem((NCH, BLK, 2 * GRP), BF16),
        vmem((NF, GRP, 256), BF16),
        vmem((NF * 128, GRP), BF16),
        vmem((NF, 2 * GRP, 256), BF16),
        vmem((2, NF * 128, GRP), BF16),
        vmem((7, NCH, 2 * BLK, 128), BF16),
        vmem((7, NCH, 2 * BLK, 128), BF16),
        vmem((NCH, NF, BLK, 128), BF16),
        vmem((3, BLK, 2 * GRP), BF16),
        vmem((3, BLK, 2 * GRP), BF16),
        vmem((BLK, 2 * GRP), F32),
        vmem((NZ, BLK, 128), F32),
        vmem((NCH, NZ, BLK, 128), BF16),
        vmem((NCH, NZ, BLK, 128), BF16),
        dma, dma((NZ,)), dma((NZ,)), dma((3,)), dma((3,)),
        dma, dma((NF,)), dma((NF,)), dma, dma, dma((NF,)), dma((NF,)),
        dma, dma, dma, dma, dma, dma, dma,
        dma((NCH, 7)), dma((NCH, 7)), dma((NCH, 7)), dma((NCH, 7)),
        dma((3,)), dma((3,)), dma((NCH, NZ)), dma((NCH, NZ)),
    ]
    return pl.pallas_call(
        kernel,
        out_shape=jax.ShapeDtypeStruct(tokens.shape, BF16),
        in_specs=[pl.BlockSpec(memory_space=pl.ANY)] * 4,
        out_specs=pl.BlockSpec(memory_space=pltpu.VMEM),
        scratch_shapes=scratch,
        compiler_params=pltpu.CompilerParams(
            collective_id=0, has_side_effects=True, vmem_limit_bytes=63 * 2**20
        ),
    )(tokens, gate_weight, up_weight, down_weight)


def solution(mesh):
    in_specs = (P("row", "col"), P("col", "row"), P("col", "row"), P("row", "col"))
    return jax.shard_map(
        per_device, mesh=mesh, in_specs=in_specs, out_specs=P("row", "col"), check_vma=False
    )
```
